32 devices in a mesh: patch: 4 (over y, x), sub: 8 (over z, core).
Axes of the slice: x: 2, y: 2, z: 4, core: 2. Of those that a mesh axis runs over, the one named last changes fastest.
Arguments:
- element_temps: float32 [16384, 64], P(('patch', 'sub')), may hold values from -6 to 6
- quad_weights: float32 [16384, 64], P(('patch', 'sub')), may hold values from 0.3 to 3
- basis_values: float32 [64, 64], replicated, may hold values from -0.75 to 0.75
- basis_grads: float32 [3, 64, 64], replicated, may hold values from -0.75 to 0.75
- owner_block: int32 [16384, 1], P(('patch', 'sub')), may hold values from 0 to 63; in each aligned block of 512 rows (0 to 511, 512 to 1023, ...) at most 16 rows name the same one
- column_ref: int32 [16384, 1], P(('patch', 'sub')), may hold values from 0 to 31
- quadrant: int32 [16384, 1], P(('patch', 'sub')), may hold values from 0 to 3
- active_counts: int32 [32], P(('patch', 'sub')), may hold values from 256 to 512, as said below
- send_list: int32 [256, 2], P(('patch', 'sub')), may hold values from 0 to 7
- iface_list: int32 [64, 4], P(('patch', 'sub')), may hold values from 0 to 7
- newton_residual: float32 [256, 128], P(('patch', 'sub')), may hold values from -6 to 6
- lumped_mass: float32 [256, 128], P(('patch', 'sub')), may hold values from 1 to 3
- precond: float32 [256, 128, 128], P(('patch', 'sub'))
Outputs:
- newton_update: float32 [256, 128], P(('patch', 'sub'))
The draws below stay inside these ranges and needn't reach their ends.
Inputs may be any that keep to these rules, and one draw needn't show every extreme that they name: `owner_block`: at most 16 elements of one device name one block, and some block is named by exactly 16 of one device's elements. `active_counts`: some device has all 512 elements active.
All inputs are finite; a program needn't handle non-finite values.
Results may differ from the reference program's by a relative error of at most 0.0001.
Values sent between devices are 32-bit elements; how exact they have to be, the bound alone decides.
A program may use at most 128 MiB of HBM per device.

```python
import math
import jax
import jax.numpy as jnp
import numpy as np
from jax import lax

Q = 64
FUNCS = 64
BPTS = 128
SWEEPS = 3
GH = 2
IG = 4
NBD = 8
NEL = 512
CAP = 16
ELEMENTS = 16384
BLOCKS = 256
NB_PATCH = 64
NX_EXT = 32
N_PATCH = 4
N_SUB = 8
DEVICES = 32


def draw_active_counts(key, part):
    first_key, second_key = jax.random.split(jax.random.fold_in(key, 11))
    counted = jax.random.randint(first_key, (DEVICES,), NEL // 2, NEL + 1)
    chosen = jax.random.randint(second_key, (), 0, DEVICES)
    return counted.at[chosen].set(NEL).astype(jnp.int32)


def draw_precond(key, part):
    noise_key = jax.random.fold_in(key, 23)
    noise = jax.random.normal(noise_key, (BLOCKS, BPTS, BPTS), jnp.float32)
    identity = jnp.eye(BPTS, dtype=jnp.float32)
    return 0.5 * (identity[None, :, :] + 0.25 * noise / 11.3137085)


def plant(drawn, stream_key, low, largest):
    longest = drawn.shape.index(max(drawn.shape))
    spots = []
    for shift in (0, 1):
        where = [jax.random.randint(jax.random.fold_in(stream_key, axis), (), 0, length) for axis, length in enumerate(drawn.shape)]
        where[longest] = (where[longest] + shift) % drawn.shape[longest]
        spots.append(tuple(where))
    return drawn.at[spots[0]].set(low).at[spots[1]].set(largest)


def level_of(rng, extent, cuts, low, high):
    gain = 1.0
    for dim, parts in cuts:
        heights = jax.random.uniform(jax.random.fold_in(jax.random.fold_in(rng, 6), dim), (parts,), jnp.float32, low / len(cuts), high / len(cuts))
        gain = gain * jnp.repeat(jnp.exp(heights), extent[dim] // parts).reshape((-1,) + (1,) * (len(extent) - 1 - dim))
    return gain


def deal_out(own_key, own, number, rows, count, top, bound, skew):
    order = jax.random.permutation(own_key, count)
    heavy_load, ordinary = portions_of(count, rows * top, bound, skew, True), portions_of(count, rows * top, bound, skew, False)
    places = jnp.arange(count)

    def named(sizes, offset_by):
        used = int((sizes > 0).sum())
        fixed = max(1, used // 4)
        passed = fixed + (places - fixed + offset_by * (used - fixed)) % max(1, count - fixed)
        return jnp.zeros((count,), jnp.int32).at[order[jnp.where(places < fixed, places, passed)]].set(jnp.asarray(sizes, jnp.int32))

    sizes = jnp.where(number % 4 == 0, named(heavy_load, number // 4), named(ordinary, number - number // 4 - 1))
    mixed = jax.random.permutation(jax.random.fold_in(own, 3), count)
    donor, taker = mixed[0:count // 2 * 2:2], mixed[1:count // 2 * 2:2]
    margin = jnp.minimum(sizes[donor] - 1, bound - sizes[taker]) // 2
    margin = jnp.where((donor == order[0]) | (taker == order[0]) | (sizes[taker] == 0), 0, jnp.maximum(margin, 0))
    passed = jax.random.randint(jax.random.fold_in(own, 4), (count // 2,), 0, 1 << 20) % (margin + 1)
    sizes = sizes.at[donor].add(-passed).at[taker].add(passed)
    labels = jnp.searchsorted(jnp.cumsum(sizes), jnp.arange(rows * top), side="right").astype(jnp.int32)
    listing = labels.reshape(top, rows).T
    listing = listing[jax.random.permutation(jax.random.fold_in(own, 1), rows)]
    offset_by = jax.random.randint(jax.random.fold_in(own, 2), (rows, 1), 0, top)
    return jnp.take_along_axis(listing, (jnp.arange(top)[None, :] + offset_by) % top, axis=1)


def portions_of(number_of, total, limit, lean, full):
    portions = [(1 << 20) // math.isqrt(grade ** lean) + 1 for grade in range(1, number_of + 1)]
    largest = limit if full else min(limit, max(-(-total // number_of), total * portions[0] // sum(portions)))
    least = 1 if total - largest >= number_of - 1 else 0
    given, spare = [largest] + [least] * (number_of - 1), total - largest - least * (number_of - 1)
    while spare > 0:
        movable = [i for i in range(1, number_of) if given[i] < largest] or [i for i in range(1, number_of) if given[i] < limit]
        mass, left = sum([portions[i] for i in movable]), spare
        for i in movable:
            more = min(limit - given[i], max(1, left * portions[i] // mass), spare)
            given[i] = given[i] + more
            spare = spare - more
    return np.array(given)


def gaussian(stream_key, shape, width, limit, cuts=(), kind=jnp.bfloat16):
    drawn = jax.random.normal(stream_key, shape, jnp.float32) * width
    if len(cuts) > 0:
        drawn = level_of(stream_key, shape, cuts, -0.22, 0.18) * drawn
    return jnp.clip(drawn, min=-limit, max=limit).astype(kind)


def setup_inputs(seed: int = 0) -> dict:
    arg_keys = jax.random.split(jax.random.key(seed), 14)
    element_temps = gaussian(arg_keys[0], (ELEMENTS, FUNCS), 1.0, 6.0, ((0, 32),), jnp.float32)
    quad_weights = jnp.clip(jnp.exp(math.log(3.0) - 2.3025851 * jax.random.uniform(arg_keys[1], (ELEMENTS, Q), jnp.float32) ** level_of(arg_keys[1], (ELEMENTS, Q), ((0, 32),), -0.2, 0.2)), 0.3, 3.0)
    basis_values = gaussian(arg_keys[2], (Q, FUNCS), FUNCS ** -0.5, 0.75, (), jnp.float32)
    basis_grads = gaussian(arg_keys[3], (3, Q, FUNCS), FUNCS ** -0.5, 0.75, (), jnp.float32)
    owner_block_keys = jax.random.split(jax.random.fold_in(arg_keys[4], 1), ELEMENTS // NEL)
    owner_block_turns = jax.random.permutation(jax.random.fold_in(arg_keys[4], 3), ELEMENTS // NEL)
    owner_block = jax.vmap(lambda own, number: deal_out(jax.random.fold_in(arg_keys[4], 2), own, number, NEL, NB_PATCH, 1, CAP, 2))(owner_block_keys, owner_block_turns).reshape((ELEMENTS, 1))
    column_ref = plant(jax.random.randint(arg_keys[5], (ELEMENTS, 1), 0, NX_EXT), jax.random.fold_in(arg_keys[5], 1), 0, NX_EXT - 1).astype(jnp.int32)
    quadrant = plant(jax.random.randint(arg_keys[6], (ELEMENTS, 1), 0, 4), jax.random.fold_in(arg_keys[6], 1), 0, 3).astype(jnp.int32)
    active_counts = draw_active_counts(jax.random.fold_in(arg_keys[13], 71), 0)
    send_list = plant(jax.random.randint(arg_keys[8], (DEVICES * N_SUB, GH), 0, NBD), jax.random.fold_in(arg_keys[8], 1), 0, NBD - 1).astype(jnp.int32)
    iface_list = plant(jax.random.randint(arg_keys[9], (DEVICES * 2, IG), 0, NBD), jax.random.fold_in(arg_keys[9], 1), 0, NBD - 1).astype(jnp.int32)
    newton_residual = gaussian(arg_keys[10], (BLOCKS, BPTS), 1.0, 6.0, ((0, 32),), jnp.float32)
    lumped_mass = jnp.clip(jnp.exp(math.log(3.0) - 1.0986123 * jax.random.uniform(arg_keys[11], (BLOCKS, BPTS), jnp.float32) ** level_of(arg_keys[11], (BLOCKS, BPTS), ((0, 32),), -0.2, 0.2)), 1.0, 3.0)
    precond = draw_precond(jax.random.fold_in(arg_keys[13], 71), 0)
    return dict(element_temps=element_temps, quad_weights=quad_weights, basis_values=basis_values, basis_grads=basis_grads, owner_block=owner_block, column_ref=column_ref, quadrant=quadrant, active_counts=active_counts, send_list=send_list, iface_list=iface_list, newton_residual=newton_residual, lumped_mass=lumped_mass, precond=precond)


highest = lax.Precision.HIGHEST
conductivity_scale = 0.005


def element_terms(element_temps, quad_weights, basis_values, basis_grads):
    values = jnp.dot(element_temps, basis_values.T, precision=highest)
    slopes = jnp.einsum("eb,cqb->ecq", element_temps, basis_grads, precision=highest)
    stiff_terms = quad_weights * conductivity_scale * (1.0 + values * values)
    newton_terms = (quad_weights * 2.0 * conductivity_scale * values)[:, None, :] * slopes
    return jnp.concatenate([stiff_terms, newton_terms.reshape(values.shape[0], -1)], axis=1)


def tile_table(basis_values, basis_grads):
    points, functions = basis_values.shape
    stiff_rows = jnp.sum(basis_grads[:, :, :, None] * basis_grads[:, :, None, :], axis=0).reshape(points, functions * functions)
    newton_rows = (basis_grads[:, :, :, None] * basis_values[None, :, None, :]).reshape(3 * points, functions * functions)
    return jnp.concatenate([stiff_rows, newton_rows], axis=0)


def reference(element_temps, quad_weights, basis_values, basis_grads, owner_block, column_ref, quadrant, active_counts, send_list, iface_list, newton_residual, lumped_mass, precond):
    products = tile_table(basis_values, basis_grads)
    functions = basis_values.shape[1]
    patch_blocks = NBD * N_SUB
    counter = jnp.arange(ELEMENTS, dtype=jnp.int32)
    device = counter // NEL
    patch_of = device // N_SUB
    within = counter % NEL
    target = owner_block[:, 0]
    owner_dev = target // NBD
    column = column_ref[:, 0]
    row_half = quadrant[:, 0] // 2
    col_half = quadrant[:, 0] % 2
    own_block = patch_of * patch_blocks + owner_dev * NBD + column
    offset = jnp.maximum(column - NBD, 0)
    source = jnp.minimum(offset // GH, N_SUB - 1)
    slot_near = offset % GH
    sub_block = patch_of * patch_blocks + source * NBD + send_list[(patch_of * N_SUB + source) * N_SUB + owner_dev, slot_near]
    far_offset = jnp.maximum(column - NBD - N_SUB * GH, 0)
    iface_side = jnp.minimum(far_offset // IG, 1)
    slot_far = far_offset % IG
    neighbour = patch_of - 1 + 2 * iface_side
    present = (neighbour >= 0) & (neighbour < N_PATCH)
    clipped = jnp.clip(neighbour, 0, N_PATCH - 1)
    far_block = clipped * patch_blocks + owner_dev * NBD + iface_list[(clipped * N_SUB + owner_dev) * 2 + 1 - iface_side, slot_far]
    is_own = column < NBD
    is_sub = column < NBD + N_SUB * GH
    col_block = jnp.where(is_own, own_block, jnp.where(is_sub, sub_block, far_block))
    enabled = (within < active_counts[device]) & (is_sub | present)
    row_seg = (patch_of * patch_blocks + target) * 2 + row_half
    col_seg = col_block * 2 + col_half
    quad_terms = element_terms(element_temps, quad_weights, basis_values, basis_grads) * enabled.astype(jnp.float32)[:, None]

    def apply_matrix(iterate):
        segments = iterate.reshape(-1, functions)

        def one_device(accum_rows, pieces):
            part_terms, part_rows, part_cols = pieces
            tile_set = jnp.dot(part_terms, products, precision=highest).reshape(-1, functions, functions)
            row_terms = jnp.einsum("rab,rb->ra", tile_set, segments[part_cols], precision=highest)
            return accum_rows.at[part_rows].add(row_terms), None

        accum_rows, unused = lax.scan(one_device, jnp.zeros(segments.shape, jnp.float32), (quad_terms.reshape(DEVICES, NEL, -1), row_seg.reshape(DEVICES, NEL), col_seg.reshape(DEVICES, NEL)))
        return accum_rows.reshape(iterate.shape)

    newton_update = jnp.einsum("bij,bj->bi", precond, newton_residual, precision=highest)
    for repeat in range(SWEEPS - 1):
        applied = lumped_mass * newton_update + apply_matrix(newton_update)
        newton_update = newton_update + jnp.einsum("bij,bj->bi", precond, newton_residual - applied, precision=highest)
    return newton_update
```

```python
import functools

import jax
import jax.numpy as jnp
from jax import lax
from jax.experimental import pallas as pl
from jax.experimental.pallas import tpu as pltpu
from jax.sharding import PartitionSpec as P

SWEEPS = 3
CONDUCTIVITY = 0.005
MESH = pl.DeviceIdType.MESH
F32 = jnp.float32
BF16 = jnp.bfloat16


def halves(x):
    head = x.astype(BF16).astype(F32)
    return head, x - head


def log2(n):
    assert n & (n - 1) == 0
    return n.bit_length() - 1


def dot(a, b):
    return jnp.dot(a, b, preferred_element_type=F32)


def dot_nt(a, b):
    return lax.dot_general(a, b, (((1,), (1,)), ((), ())), preferred_element_type=F32)


def kernel(
    dims,
    temps,
    weights,
    values,
    grads,
    owner,
    column,
    quadrant,
    counts,
    sends,
    ifaces,
    residual,
    mass,
    precond,
    out,
    ext,
    ifb,
    ub,
    rows_out,
    rows_in,
    pick,
    put,
    terms,
    ph,
    plo,
    ag_send,
    ag_recv,
    if_send,
    if_recv,
    rs_send,
    rs_recv,
):
    n_patch, n_sub, nbd, gh, ig, erows, base, nbp, rbp = dims
    patch, sub = lax.axis_index("patch"), lax.axis_index("sub")
    upper = lax.rem(patch + 1, n_patch)
    lower = lax.rem(patch + n_patch - 1, n_patch)
    peers = [lax.rem(sub + k, n_sub) for k in range(1, n_sub)]
    sources = [lax.rem(sub + n_sub - k, n_sub) for k in range(1, n_sub)]
    everyone = [lax.rem(sub + k, n_sub) for k in range(n_sub)]

    barrier = pltpu.get_barrier_semaphore()
    for peer in peers:
        pl.semaphore_signal(barrier, inc=1, device_id=(patch, peer), device_id_type=MESH)
    for other in (upper, lower):
        for peer in everyone:
            pl.semaphore_signal(barrier, inc=1, device_id=(other, peer), device_id_type=MESH)

    def solve(r):
        head, rest = halves(r)
        both = jnp.concatenate([head, rest], axis=0).astype(BF16)
        wide = dot_nt(both, ph[...]) + dot_nt(both, plo[...])
        wide = wide[:nbd] + wide[nbd:]
        row = lax.broadcasted_iota(jnp.int32, (nbd, 128), 0)
        total = jnp.zeros((nbd, 128), F32)
        for b in range(nbd):
            total = total + jnp.where(row == b, wide[:, b * 128 : (b + 1) * 128], 0.0)
        return total

    def expand(u, sweep):
        ub[sweep] = u
        first = pl.multiple_of(sub * erows, 8)
        ext[sweep, pl.ds(first, nbd), :] = u
        for o in range(n_sub):
            for j in range(gh):
                ext[sweep, pl.ds(first + (nbd + o * gh + j), 1), :] = ub[
                    sweep, pl.ds(sends[j, o], 1), :
                ]
        for side in range(2):
            for j in range(ig):
                ifb[sweep, pl.ds(side * ig + j, 1), :] = ub[sweep, pl.ds(ifaces[side, j], 1), :]

    def spread(sweep):
        copies = []
        mine = pl.ds(pl.multiple_of(sub * erows, 8), erows)
        for side, other in ((0, upper), (1, lower)):
            place = pl.ds(pl.multiple_of(base + (side * n_sub + sub) * 2 * ig, 8), 2 * ig)
            for k, peer in enumerate(everyone):
                copies.append(
                    pltpu.make_async_remote_copy(
                        src_ref=ifb.at[sweep],
                        dst_ref=ext.at[sweep, place],
                        send_sem=if_send.at[sweep, side, k],
                        recv_sem=if_recv.at[sweep, side, sub],
                        device_id=(other, peer),
                        device_id_type=MESH,
                    )
                )
        for k, peer in enumerate(peers):
            copies.append(
                pltpu.make_async_remote_copy(
                    src_ref=ext.at[sweep, mine],
                    dst_ref=ext.at[sweep, mine],
                    send_sem=ag_send.at[sweep, k],
                    recv_sem=ag_recv.at[sweep, sub],
                    device_id=(patch, peer),
                    device_id_type=MESH,
                )
            )
        for copy in copies:
            copy.start()
        return copies

    def gathered(sweep):
        for k, source in enumerate(sources):
            place = pl.ds(pl.multiple_of(source * erows, 8), erows)
            pltpu.make_async_remote_copy(
                src_ref=ext.at[sweep, place],
                dst_ref=ext.at[sweep, place],
                send_sem=ag_send.at[sweep, k],
                recv_sem=ag_recv.at[sweep, source],
                device_id=(patch, source),
                device_id_type=MESH,
            ).wait_recv()
        for side in range(2):
            for s in range(n_sub):
                pltpu.make_async_remote_copy(
                    src_ref=ifb.at[sweep],
                    dst_ref=ext.at[sweep, pl.ds(base + (side * n_sub + s) * 2 * ig, 2 * ig)],
                    send_sem=if_send.at[sweep, side, s],
                    recv_sem=if_recv.at[sweep, side, s],
                    device_id=(lower, s),
                    device_id_type=MESH,
                ).wait_recv()

    r = residual[...]
    p_all = precond[...].reshape(nbd * 128, 128)
    p_head = p_all.astype(BF16)
    ph[...] = p_head
    plo[...] = (p_all - p_head.astype(F32)).astype(BF16)
    used = base + 4 * ig * n_sub
    if nbp > used:
        for sweep in range(SWEEPS - 1):
            ext[sweep, pl.ds(used, nbp - used), :] = jnp.zeros((nbp - used, 128), F32)
    u = solve(r)
    expand(u, 0)
    pl.semaphore_wait(barrier, n_sub - 1 + 2 * n_sub)
    copies = spread(0)

    points, functions = values.shape
    elements = temps.shape[1]
    g3 = grads[...].reshape(3 * points, functions)
    g_head, g_rest = halves(jnp.concatenate([g3, values[...]], axis=0))
    left = jnp.concatenate([g_head, g_head, g_rest, g_rest], axis=1).astype(BF16)
    h3, l3 = g_head[: 3 * points], g_rest[: 3 * points]
    back = jnp.transpose(jnp.concatenate([h3, h3, l3, l3], axis=0)).astype(BF16)
    t_head, t_rest = halves(temps[...])
    four = jnp.concatenate([t_head, t_rest, t_head, t_rest], axis=0).astype(BF16)
    fields = dot(left, four)
    vals = fields[3 * points :]
    w = weights[...]
    terms[pl.ds(0, points), :] = w * CONDUCTIVITY * (1.0 + vals * vals)
    slope_weight = w * (2.0 * CONDUCTIVITY) * vals
    for c in range(3):
        terms[pl.ds((c + 1) * points, points), :] = (
            slope_weight * fields[c * points : (c + 1) * points]
        )
    block, col, quad = owner[...], column[...], quadrant[...]
    o = block >> log2(nbd)
    near = col - nbd
    far = near - n_sub * gh
    side = far >> log2(ig)
    own_place = o * erows + col
    near_place = (near >> log2(gh)) * erows + nbd + o * gh + (near & (gh - 1))
    far_place = base + (side * n_sub + o) * 2 * ig + (1 - side) * ig + (far & (ig - 1))
    neighbour = patch - 1 + 2 * side
    far_place = jnp.where((neighbour >= 0) & (neighbour < n_patch), far_place, -2 * nbp)
    place = jnp.where(near < 0, own_place, jnp.where(far < 0, near_place, far_place))
    place = place + (quad & 1) * nbp
    active = lax.broadcasted_iota(jnp.int32, (1, elements), 1) < counts[0]
    target = jnp.where(active, block + (quad >> 1) * rbp, -1)
    for i in range(2 * nbp // 128):
        index = lax.broadcasted_iota(jnp.int32, (128, elements), 0) + i * 128
        pick[pl.ds(i * 128, 128), :] = jnp.where(index == place, 1.0, 0.0).astype(BF16)
    for i in range(2 * rbp // 128):
        index = lax.broadcasted_iota(jnp.int32, (128, elements), 0) + i * 128
        put[pl.ds(i * 128, 128), :] = jnp.where(index == target, 1.0, 0.0).astype(BF16)

    for sweep in range(SWEEPS - 1):
        gathered(sweep)
        flat = jnp.transpose(ext[sweep])
        head, rest = halves(flat)
        segments = jnp.concatenate(
            [
                jnp.concatenate([head[:functions], head[functions:]], axis=1),
                jnp.concatenate([rest[:functions], rest[functions:]], axis=1),
            ],
            axis=0,
        ).astype(BF16)
        x = dot(segments, pick[...]).astype(BF16)
        gx = dot(left, jnp.concatenate([x, x], axis=0))
        vx = gx[3 * points :]
        k0 = terms[pl.ds(0, points), :]
        flux = jnp.concatenate(
            [
                k0 * gx[c * points : (c + 1) * points]
                + terms[pl.ds((c + 1) * points, points), :] * vx
                for c in range(3)
            ],
            axis=0,
        )
        f_head, f_rest = halves(flux)
        z = dot_nt(jnp.concatenate([f_head, f_rest], axis=0).astype(BF16), put[...])
        z_head, z_rest = halves(z[: 3 * points] + z[3 * points :])
        rt = dot(back, jnp.concatenate([z_head, z_rest, z_head, z_rest], axis=0).astype(BF16))
        rows_out[sweep] = jnp.transpose(jnp.concatenate([rt[:, :rbp], rt[:, rbp:]], axis=0))
        for k, peer in enumerate(peers):
            copy = pltpu.make_async_remote_copy(
                src_ref=rows_out.at[sweep, pl.ds(pl.multiple_of(peer * nbd, 8), nbd)],
                dst_ref=rows_in.at[sweep, sub],
                send_sem=rs_send.at[sweep, k],
                recv_sem=rs_recv.at[sweep, sub],
                device_id=(patch, peer),
                device_id_type=MESH,
            )
            copy.start()
            copies.append(copy)
        applied = mass[...] * u + rows_out[sweep, pl.ds(pl.multiple_of(sub * nbd, 8), nbd), :]
        for k, source in enumerate(sources):
            pltpu.make_async_remote_copy(
                src_ref=rows_in.at[sweep, source],
                dst_ref=rows_in.at[sweep, source],
                send_sem=rs_send.at[sweep, k],
                recv_sem=rs_recv.at[sweep, source],
                device_id=(patch, source),
                device_id_type=MESH,
            ).wait_recv()
            applied = applied + rows_in[sweep, source]
        u = u + solve(r - applied)
        if sweep < SWEEPS - 2:
            expand(u, sweep + 1)
            copies += spread(sweep + 1)
    out[...] = u
    for copy in copies:
        copy.wait_send()


def body(
    element_temps,
    quad_weights,
    basis_values,
    basis_grads,
    owner_block,
    column_ref,
    quadrant,
    active_counts,
    send_list,
    iface_list,
    newton_residual,
    lumped_mass,
    precond,
):
    n_patch, n_sub = lax.axis_size("patch"), lax.axis_size("sub")
    nbd, points = newton_residual.shape
    gh, ig = send_list.shape[1], iface_list.shape[1]
    elements = element_temps.shape[0]
    quads = basis_values.shape[0]
    erows = -(-(nbd + n_sub * gh) // 8) * 8
    base = n_sub * erows
    nbp = -(-(base + 4 * ig * n_sub) // 128) * 128
    rbp = -(-(n_sub * nbd) // 128) * 128
    dims = (n_patch, n_sub, nbd, gh, ig, erows, base, nbp, rbp)
    steps = SWEEPS - 1
    vmem = pl.BlockSpec(memory_space=pltpu.VMEM)
    smem = pl.BlockSpec(memory_space=pltpu.SMEM)
    dma = pltpu.SemaphoreType.DMA
    return pl.pallas_call(
        functools.partial(kernel, dims),
        out_shape=jax.ShapeDtypeStruct((nbd, points), F32),
        in_specs=[vmem] * 7 + [smem] * 3 + [vmem] * 3,
        out_specs=vmem,
        scratch_shapes=[
            pltpu.VMEM((steps, nbp, points), F32),
            pltpu.VMEM((steps, 2 * ig, points), F32),
            pltpu.VMEM((steps, nbd, points), F32),
            pltpu.VMEM((steps, rbp, points), F32),
            pltpu.VMEM((steps, n_sub, nbd, points), F32),
            pltpu.VMEM((2 * nbp, elements), BF16),
            pltpu.VMEM((2 * rbp, elements), BF16),
            pltpu.VMEM((4 * quads, elements), F32),
            pltpu.VMEM((nbd * points, points), BF16),
            pltpu.VMEM((nbd * points, points), BF16),
            dma((steps, n_sub)),
            dma((steps, n_sub)),
            dma((steps, 2, n_sub)),
            dma((steps, 2, n_sub)),
            dma((steps, n_sub)),
            dma((steps, n_sub)),
        ],
        compiler_params=pltpu.CompilerParams(
            collective_id=0, has_side_effects=True, vmem_limit_bytes=32 * 1024 * 1024
        ),
    )(
        element_temps.T,
        quad_weights.T,
        basis_values,
        basis_grads,
        owner_block.reshape(1, elements),
        column_ref.reshape(1, elements),
        quadrant.reshape(1, elements),
        active_counts,
        send_list.T,
        iface_list,
        newton_residual,
        lumped_mass,
        precond,
    )


def solution(mesh):
    return jax.shard_map(
        body,
        mesh=mesh,
        in_specs=(
            P(("patch", "sub"), None),
            P(("patch", "sub"), None),
            P(),
            P(),
            P(("patch", "sub"), None),
            P(("patch", "sub"), None),
            P(("patch", "sub"), None),
            P(("patch", "sub")),
            P(("patch", "sub"), None),
            P(("patch", "sub"), None),
            P(("patch", "sub"), None),
            P(("patch", "sub"), None),
            P(("patch", "sub"), None, None),
        ),
        out_specs=P(("patch", "sub"), None),
        check_vma=False,
    )
```

```python
import functools

import jax
import jax.numpy as jnp
from jax import lax
from jax.experimental import pallas as pl
from jax.experimental.pallas import tpu as pltpu
from jax.sharding import PartitionSpec as P

SWEEPS = 3
CONDUCTIVITY = 0.005
MESH = pl.DeviceIdType.MESH
F32 = jnp.float32
BF16 = jnp.bfloat16


def halves(x):
    head = x.astype(BF16).astype(F32)
    return head, x - head


def log2(n):
    assert n & (n - 1) == 0
    return n.bit_length() - 1


def dot(a, b):
    return jnp.dot(a, b, preferred_element_type=F32)


def dot_nt(a, b):
    return lax.dot_general(a, b, (((1,), (1,)), ((), ())), preferred_element_type=F32)


def kernel(
    dims,
    temps_in,
    weights_in,
    values_in,
    grads_in,
    owner_in,
    column_in,
    quadrant_in,
    counts_in,
    sends_in,
    ifaces_in,
    residual_in,
    mass_in,
    precond_in,
    out,
    temps,
    weights,
    values,
    grads,
    owner,
    column,
    quadrant,
    counts,
    sends,
    ifaces,
    residual,
    mass,
    precond,
    load_sem,
    ext,
    ifb,
    ub,
    rows_out,
    rows_in,
    pick,
    put,
    terms,
    ph,
    plo,
    ag_send,
    ag_recv,
    if_send,
    if_recv,
    rs_send,
    rs_recv,
):
    n_patch, n_sub, nbd, gh, ig, erows, base, nbp, rbp = dims
    patch, sub = lax.axis_index("patch"), lax.axis_index("sub")
    upper = lax.rem(patch + 1, n_patch)
    lower = lax.rem(patch + n_patch - 1, n_patch)
    peers = [lax.rem(sub + k, n_sub) for k in range(1, n_sub)]
    sources = [lax.rem(sub + n_sub - k, n_sub) for k in range(1, n_sub)]
    everyone = [lax.rem(sub + k, n_sub) for k in range(n_sub)]

    pairs = (
        (residual_in, residual),
        (sends_in, sends),
        (ifaces_in, ifaces),
        (precond_in, precond),
        (temps_in, temps),
        (grads_in, grads),
        (values_in, values),
        (weights_in, weights),
        (owner_in, owner),
        (column_in, column),
        (quadrant_in, quadrant),
        (counts_in, counts),
        (mass_in, mass),
    )
    loads = [
        pltpu.make_async_copy(given, held, load_sem.at[i]) for i, (given, held) in enumerate(pairs)
    ]
    for load in loads:
        load.start()
    barrier = pltpu.get_barrier_semaphore()
    for peer in peers:
        pl.semaphore_signal(barrier, inc=1, device_id=(patch, peer), device_id_type=MESH)
    for other in (upper, lower):
        for peer in everyone:
            pl.semaphore_signal(barrier, inc=1, device_id=(other, peer), device_id_type=MESH)

    def solve(r):
        head, rest = halves(r)
        both = jnp.concatenate([head, rest], axis=0).astype(BF16)
        wide = dot_nt(both, ph[...]) + dot_nt(both, plo[...])
        wide = wide[:nbd] + wide[nbd:]
        row = lax.broadcasted_iota(jnp.int32, (nbd, 128), 0)
        total = jnp.zeros((nbd, 128), F32)
        for b in range(nbd):
            total = total + jnp.where(row == b, wide[:, b * 128 : (b + 1) * 128], 0.0)
        return total

    def expand(u, sweep):
        ub[sweep] = u
        first = pl.multiple_of(sub * erows, 8)
        ext[sweep, pl.ds(first, nbd), :] = u
        for o in range(n_sub):
            for j in range(gh):
                ext[sweep, pl.ds(first + (nbd + o * gh + j), 1), :] = ub[
                    sweep, pl.ds(sends[j, o], 1), :
                ]
        for side in range(2):
            for j in range(ig):
                ifb[sweep, pl.ds(side * ig + j, 1), :] = ub[sweep, pl.ds(ifaces[side, j], 1), :]

    def spread(sweep):
        copies = []
        mine = pl.ds(pl.multiple_of(sub * erows, 8), erows)
        for side, other in ((0, upper), (1, lower)):
            place = pl.ds(pl.multiple_of(base + (side * n_sub + sub) * 2 * ig, 8), 2 * ig)
            for k, peer in enumerate(everyone):
                copies.append(
                    pltpu.make_async_remote_copy(
                        src_ref=ifb.at[sweep],
                        dst_ref=ext.at[sweep, place],
                        send_sem=if_send.at[sweep, side, k],
                        recv_sem=if_recv.at[sweep, side, sub],
                        device_id=(other, peer),
                        device_id_type=MESH,
                    )
                )
        for k, peer in enumerate(peers):
            copies.append(
                pltpu.make_async_remote_copy(
                    src_ref=ext.at[sweep, mine],
                    dst_ref=ext.at[sweep, mine],
                    send_sem=ag_send.at[sweep, k],
                    recv_sem=ag_recv.at[sweep, sub],
                    device_id=(patch, peer),
                    device_id_type=MESH,
                )
            )
        for copy in copies:
            copy.start()
        return copies

    def gathered(sweep):
        for k, source in enumerate(sources):
            place = pl.ds(pl.multiple_of(source * erows, 8), erows)
            pltpu.make_async_remote_copy(
                src_ref=ext.at[sweep, place],
                dst_ref=ext.at[sweep, place],
                send_sem=ag_send.at[sweep, k],
                recv_sem=ag_recv.at[sweep, source],
                device_id=(patch, source),
                device_id_type=MESH,
            ).wait_recv()
        for side in range(2):
            for s in range(n_sub):
                pltpu.make_async_remote_copy(
                    src_ref=ifb.at[sweep],
                    dst_ref=ext.at[sweep, pl.ds(base + (side * n_sub + s) * 2 * ig, 2 * ig)],
                    send_sem=if_send.at[sweep, side, s],
                    recv_sem=if_recv.at[sweep, side, s],
                    device_id=(lower, s),
                    device_id_type=MESH,
                ).wait_recv()

    for load in loads[:4]:
        load.wait()
    r = residual[...]
    p_all = precond[...].reshape(nbd * 128, 128)
    p_head = p_all.astype(BF16)
    ph[...] = p_head
    plo[...] = (p_all - p_head.astype(F32)).astype(BF16)
    used = base + 4 * ig * n_sub
    if nbp > used:
        for sweep in range(SWEEPS - 1):
            ext[sweep, pl.ds(used, nbp - used), :] = jnp.zeros((nbp - used, 128), F32)
    u = solve(r)
    expand(u, 0)
    pl.semaphore_wait(barrier, n_sub - 1 + 2 * n_sub)
    copies = spread(0)

    for load in loads[4:]:
        load.wait()
    points, functions = values.shape
    elements = temps.shape[1]
    g3 = grads[...].reshape(3 * points, functions)
    g_head, g_rest = halves(jnp.concatenate([g3, values[...]], axis=0))
    left = jnp.concatenate([g_head, g_head, g_rest, g_rest], axis=1).astype(BF16)
    h3, l3 = g_head[: 3 * points], g_rest[: 3 * points]
    back = jnp.transpose(jnp.concatenate([h3, h3, l3, l3], axis=0)).astype(BF16)
    t_head, t_rest = halves(temps[...])
    four = jnp.concatenate([t_head, t_rest, t_head, t_rest], axis=0).astype(BF16)
    fields = dot(left, four)
    vals = fields[3 * points :]
    w = weights[...]
    terms[pl.ds(0, points), :] = w * CONDUCTIVITY * (1.0 + vals * vals)
    slope_weight = w * (2.0 * CONDUCTIVITY) * vals
    for c in range(3):
        terms[pl.ds((c + 1) * points, points), :] = (
            slope_weight * fields[c * points : (c + 1) * points]
        )
    block, col, quad = owner[...], column[...], quadrant[...]
    o = block >> log2(nbd)
    near = col - nbd
    far = near - n_sub * gh
    side = far >> log2(ig)
    own_place = o * erows + col
    near_place = (near >> log2(gh)) * erows + nbd + o * gh + (near & (gh - 1))
    far_place = base + (side * n_sub + o) * 2 * ig + (1 - side) * ig + (far & (ig - 1))
    neighbour = patch - 1 + 2 * side
    far_place = jnp.where((neighbour >= 0) & (neighbour < n_patch), far_place, -2 * nbp)
    place = jnp.where(near < 0, own_place, jnp.where(far < 0, near_place, far_place))
    place = place + (quad & 1) * nbp
    active = lax.broadcasted_iota(jnp.int32, (1, elements), 1) < counts[...]
    target = jnp.where(active, block + (quad >> 1) * rbp, -1)
    for i in range(2 * nbp // 128):
        index = lax.broadcasted_iota(jnp.int32, (128, elements), 0) + i * 128
        pick[pl.ds(i * 128, 128), :] = jnp.where(index == place, 1.0, 0.0).astype(BF16)
    for i in range(2 * rbp // 128):
        index = lax.broadcasted_iota(jnp.int32, (128, elements), 0) + i * 128
        put[pl.ds(i * 128, 128), :] = jnp.where(index == target, 1.0, 0.0).astype(BF16)

    for sweep in range(SWEEPS - 1):
        gathered(sweep)
        flat = jnp.transpose(ext[sweep])
        head, rest = halves(flat)
        segments = jnp.concatenate(
            [
                jnp.concatenate([head[:functions], head[functions:]], axis=1),
                jnp.concatenate([rest[:functions], rest[functions:]], axis=1),
            ],
            axis=0,
        ).astype(BF16)
        x = dot(segments, pick[...]).astype(BF16)
        gx = dot(left, jnp.concatenate([x, x], axis=0))
        vx = gx[3 * points :]
        k0 = terms[pl.ds(0, points), :]
        flux = jnp.concatenate(
            [
                k0 * gx[c * points : (c + 1) * points]
                + terms[pl.ds((c + 1) * points, points), :] * vx
                for c in range(3)
            ],
            axis=0,
        )
        f_head, f_rest = halves(flux)
        z = dot_nt(jnp.concatenate([f_head, f_rest], axis=0).astype(BF16), put[...])
        z_head, z_rest = halves(z[: 3 * points] + z[3 * points :])
        rt = dot(back, jnp.concatenate([z_head, z_rest, z_head, z_rest], axis=0).astype(BF16))
        rows_out[sweep] = jnp.transpose(jnp.concatenate([rt[:, :rbp], rt[:, rbp:]], axis=0))
        for k, peer in enumerate(peers):
            copy = pltpu.make_async_remote_copy(
                src_ref=rows_out.at[sweep, pl.ds(pl.multiple_of(peer * nbd, 8), nbd)],
                dst_ref=rows_in.at[sweep, sub],
                send_sem=rs_send.at[sweep, k],
                recv_sem=rs_recv.at[sweep, sub],
                device_id=(patch, peer),
                device_id_type=MESH,
            )
            copy.start()
            copies.append(copy)
        applied = mass[...] * u + rows_out[sweep, pl.ds(pl.multiple_of(sub * nbd, 8), nbd), :]
        for k, source in enumerate(sources):
            pltpu.make_async_remote_copy(
                src_ref=rows_in.at[sweep, source],
                dst_ref=rows_in.at[sweep, source],
                send_sem=rs_send.at[sweep, k],
                recv_sem=rs_recv.at[sweep, source],
                device_id=(patch, source),
                device_id_type=MESH,
            ).wait_recv()
            applied = applied + rows_in[sweep, source]
        u = u + solve(r - applied)
        if sweep < SWEEPS - 2:
            expand(u, sweep + 1)
            copies += spread(sweep + 1)
    out[...] = u
    for copy in copies:
        copy.wait_send()


def body(
    element_temps,
    quad_weights,
    basis_values,
    basis_grads,
    owner_block,
    column_ref,
    quadrant,
    active_counts,
    send_list,
    iface_list,
    newton_residual,
    lumped_mass,
    precond,
):
    n_patch, n_sub = lax.axis_size("patch"), lax.axis_size("sub")
    nbd, points = newton_residual.shape
    gh, ig = send_list.shape[1], iface_list.shape[1]
    elements = element_temps.shape[0]
    quads = basis_values.shape[0]
    erows = -(-(nbd + n_sub * gh) // 8) * 8
    base = n_sub * erows
    nbp = -(-(base + 4 * ig * n_sub) // 128) * 128
    rbp = -(-(n_sub * nbd) // 128) * 128
    dims = (n_patch, n_sub, nbd, gh, ig, erows, base, nbp, rbp)
    steps = SWEEPS - 1
    vmem = pl.BlockSpec(memory_space=pltpu.VMEM)
    hbm = pl.BlockSpec(memory_space=pltpu.HBM)
    dma = pltpu.SemaphoreType.DMA
    return pl.pallas_call(
        functools.partial(kernel, dims),
        out_shape=jax.ShapeDtypeStruct((nbd, points), F32),
        in_specs=[hbm] * 13,
        out_specs=vmem,
        scratch_shapes=[
            pltpu.VMEM(element_temps.shape[::-1], F32),
            pltpu.VMEM(quad_weights.shape[::-1], F32),
            pltpu.VMEM(basis_values.shape, F32),
            pltpu.VMEM(basis_grads.shape, F32),
            pltpu.VMEM((1, elements), jnp.int32),
            pltpu.VMEM((1, elements), jnp.int32),
            pltpu.VMEM((1, elements), jnp.int32),
            pltpu.VMEM((1, 1), jnp.int32),
            pltpu.SMEM(send_list.shape[::-1], jnp.int32),
            pltpu.SMEM(iface_list.shape, jnp.int32),
            pltpu.VMEM(newton_residual.shape, F32),
            pltpu.VMEM(lumped_mass.shape, F32),
            pltpu.VMEM(precond.shape, F32),
            dma((13,)),
            pltpu.VMEM((steps, nbp, points), F32),
            pltpu.VMEM((steps, 2 * ig, points), F32),
            pltpu.VMEM((steps, nbd, points), F32),
            pltpu.VMEM((steps, rbp, points), F32),
            pltpu.VMEM((steps, n_sub, nbd, points), F32),
            pltpu.VMEM((2 * nbp, elements), BF16),
            pltpu.VMEM((2 * rbp, elements), BF16),
            pltpu.VMEM((4 * quads, elements), F32),
            pltpu.VMEM((nbd * points, points), BF16),
            pltpu.VMEM((nbd * points, points), BF16),
            dma((steps, n_sub)),
            dma((steps, n_sub)),
            dma((steps, 2, n_sub)),
            dma((steps, 2, n_sub)),
            dma((steps, n_sub)),
            dma((steps, n_sub)),
        ],
        compiler_params=pltpu.CompilerParams(
            collective_id=0, has_side_effects=True, vmem_limit_bytes=56 * 1024 * 1024
        ),
    )(
        element_temps.T,
        quad_weights.T,
        basis_values,
        basis_grads,
        owner_block.reshape(1, elements),
        column_ref.reshape(1, elements),
        quadrant.reshape(1, elements),
        active_counts.reshape(1, 1),
        send_list.T,
        iface_list,
        newton_residual,
        lumped_mass,
        precond,
    )


def solution(mesh):
    return jax.shard_map(
        body,
        mesh=mesh,
        in_specs=(
            P(("patch", "sub"), None),
            P(("patch", "sub"), None),
            P(),
            P(),
            P(("patch", "sub"), None),
            P(("patch", "sub"), None),
            P(("patch", "sub"), None),
            P(("patch", "sub")),
            P(("patch", "sub"), None),
            P(("patch", "sub"), None),
            P(("patch", "sub"), None),
            P(("patch", "sub"), None),
            P(("patch", "sub"), None, None),
        ),
        out_specs=P(("patch", "sub"), None),
        check_vma=False,
    )
```

```python
import functools

import jax
import jax.numpy as jnp
from jax import lax
from jax.experimental import pallas as pl
from jax.experimental.pallas import tpu as pltpu
from jax.sharding import PartitionSpec as P

SWEEPS = 3
CONDUCTIVITY = 0.005
MESH = pl.DeviceIdType.MESH
F32 = jnp.float32
BF16 = jnp.bfloat16


def halves(x):
    head = x.astype(BF16).astype(F32)
    return head, x - head


def log2(n):
    assert n & (n - 1) == 0
    return n.bit_length() - 1


def dot(a, b):
    return jnp.dot(a, b, preferred_element_type=F32)


def dot_nt(a, b):
    return lax.dot_general(a, b, (((1,), (1,)), ((), ())), preferred_element_type=F32)


def kernel(
    dims,
    temps_in,
    weights_in,
    values_in,
    grads_in,
    owner_in,
    column_in,
    quadrant_in,
    counts_in,
    sends_in,
    ifaces_in,
    residual_in,
    mass_in,
    precond_in,
    out,
    temps,
    weights,
    values,
    grads,
    owner,
    column,
    quadrant,
    counts,
    sends,
    ifaces,
    residual,
    mass,
    precond,
    load_sem,
    ext,
    ifb,
    rows_out,
    rows_in,
    pick,
    put,
    terms,
    ph,
    plo,
    ag_send,
    ag_recv,
    if_send,
    if_recv,
    rs_send,
    rs_recv,
):
    n_patch, n_sub, nbd, gh, ig, erows, base, ifp, rbp = dims
    patch, sub = lax.axis_index("patch"), lax.axis_index("sub")
    upper = lax.rem(patch + 1, n_patch)
    lower = lax.rem(patch + n_patch - 1, n_patch)
    steps = sorted(range(n_sub), key=lambda k: (abs(k - n_sub // 2), k))
    has = (patch < n_patch - 1, patch > 0)
    neighbours = jnp.where(has[0], n_sub, 0) + jnp.where(has[1], n_sub, 0)
    peers = [lax.rem(sub + k, n_sub) for k in steps if k]
    sources = [lax.rem(sub + n_sub - k, n_sub) for k in range(1, n_sub)]
    everyone = [lax.rem(sub + k, n_sub) for k in steps]

    far_rows = 2 * ig * n_sub
    for side in range(2):
        for s in range(n_sub):
            for sweep in range(SWEEPS - 1):
                ext[sweep, pl.ds(base + (side * n_sub + s) * 2 * ig + side * ig, ig), :] = (
                    jnp.zeros((ig, 128), F32)
                )

        @pl.when(jnp.logical_not(has[1 - side]))
        def clear():
            for sweep in range(SWEEPS - 1):
                ext[sweep, pl.ds(base + side * far_rows, far_rows), :] = jnp.zeros(
                    (far_rows, 128), F32
                )

    barrier = pltpu.get_barrier_semaphore()
    for side, other in ((0, upper), (1, lower)):

        @pl.when(has[side])
        def greet():
            for peer in everyone:
                pl.semaphore_signal(barrier, inc=1, device_id=(other, peer), device_id_type=MESH)

    for peer in peers:
        pl.semaphore_signal(barrier, inc=1, device_id=(patch, peer), device_id_type=MESH)
    pairs = (
        (residual_in, residual),
        (sends_in, sends),
        (ifaces_in, ifaces),
        (precond_in, precond),
        (temps_in, temps),
        (grads_in, grads),
        (values_in, values),
        (weights_in, weights),
        (owner_in, owner),
        (column_in, column),
        (quadrant_in, quadrant),
        (counts_in, counts),
        (mass_in, mass),
    )
    loads = [
        pltpu.make_async_copy(given, held, load_sem.at[i]) for i, (given, held) in enumerate(pairs)
    ]
    for load in loads:
        load.start()

    def solve(r):
        head, rest = halves(r)
        both = jnp.concatenate([head, rest], axis=0).astype(BF16)
        wide = dot_nt(both, ph[...]) + dot_nt(both, plo[...])
        wide = wide[:nbd] + wide[nbd:]
        row = lax.broadcasted_iota(jnp.int32, (nbd, 128), 0)
        total = jnp.zeros((nbd, 128), F32)
        for b in range(nbd):
            total = total + jnp.where(row == b, wide[:, b * 128 : (b + 1) * 128], 0.0)
        return total

    def listed(scalars, rows):
        row = lax.broadcasted_iota(jnp.int32, (rows, 128), 0)
        index = jnp.full((rows, 128), -1, jnp.int32)
        for i, scalar in enumerate(scalars):
            index = jnp.where(row == i, scalar, index)
        return index

    def choose(u, index):
        chosen = jnp.zeros(index.shape, F32)
        for b in range(nbd):
            chosen = jnp.where(index == b, u[b : b + 1], chosen)
        return chosen

    def expand(u, sweep):
        first = pl.multiple_of(sub * erows, 8)
        ext[sweep, pl.ds(first, nbd), :] = u
        ext[sweep, pl.ds(first + nbd, erows - nbd), :] = choose(u, send_index)
        ifb[sweep] = choose(u, iface_index)

    def far_copies(sweep, side, other):
        place = pl.ds(base + (side * n_sub + sub) * 2 * ig + (1 - side) * ig, ig)
        listed_rows = pl.ds((1 - side) * ig, ig)
        return [
            pltpu.make_async_remote_copy(
                src_ref=ifb.at[sweep, listed_rows],
                dst_ref=ext.at[sweep, place],
                send_sem=if_send.at[sweep, side, k],
                recv_sem=if_recv.at[sweep, side, sub],
                device_id=(other, peer),
                device_id_type=MESH,
            )
            for k, peer in enumerate(everyone)
        ]

    def far_each(sweep, act):
        for side, other in ((0, upper), (1, lower)):

            @pl.when(has[side])
            def run():
                for copy in far_copies(sweep, side, other):
                    act(copy)

    def spread(sweep):
        mine = pl.ds(pl.multiple_of(sub * erows, 8), erows)
        far_each(sweep, lambda copy: copy.start())
        copies = [
            pltpu.make_async_remote_copy(
                src_ref=ext.at[sweep, mine],
                dst_ref=ext.at[sweep, mine],
                send_sem=ag_send.at[sweep, k],
                recv_sem=ag_recv.at[sweep, sub],
                device_id=(patch, peer),
                device_id_type=MESH,
            )
            for k, peer in enumerate(peers)
        ]
        for copy in copies:
            copy.start()
        return copies

    def gathered(sweep):
        for k, source in enumerate(sources):
            place = pl.ds(pl.multiple_of(source * erows, 8), erows)
            pltpu.make_async_remote_copy(
                src_ref=ext.at[sweep, place],
                dst_ref=ext.at[sweep, place],
                send_sem=ag_send.at[sweep, k],
                recv_sem=ag_recv.at[sweep, source],
                device_id=(patch, source),
                device_id_type=MESH,
            ).wait_recv()

    def gathered_far(sweep):
        for side in range(2):

            @pl.when(has[1 - side])
            def arrive():
                for s in range(n_sub):
                    pltpu.make_async_remote_copy(
                        src_ref=ifb.at[sweep, pl.ds((1 - side) * ig, ig)],
                        dst_ref=ext.at[sweep, pl.ds(base + (side * n_sub + s) * 2 * ig + (1 - side) * ig, ig)],
                        send_sem=if_send.at[sweep, side, s],
                        recv_sem=if_recv.at[sweep, side, s],
                        device_id=(patch, s),
                        device_id_type=MESH,
                    ).wait_recv()

    def segments(sweep, first, count):
        flat = jnp.transpose(ext[sweep, pl.ds(first, count), :])
        head, rest = halves(flat)
        size = flat.shape[0] // 2
        return jnp.concatenate(
            [
                jnp.concatenate([head[:size], head[size:]], axis=1),
                jnp.concatenate([rest[:size], rest[size:]], axis=1),
            ],
            axis=0,
        ).astype(BF16)

    for load in loads[:4]:
        load.wait()
    r = residual[...]
    p_all = precond[...].reshape(nbd * 128, 128)
    p_head = p_all.astype(BF16)
    ph[...] = p_head
    plo[...] = (p_all - p_head.astype(F32)).astype(BF16)
    for first, end in ((n_sub * erows, base), (base + 4 * ig * n_sub, base + ifp)):
        if end > first:
            for sweep in range(SWEEPS - 1):
                ext[sweep, pl.ds(first, end - first), :] = jnp.zeros((end - first, 128), F32)
    send_index = listed([sends[j, o] for o in range(n_sub) for j in range(gh)], erows - nbd)
    iface_index = listed([ifaces[side, j] for side in range(2) for j in range(ig)], 2 * ig)
    u = solve(r)
    expand(u, 0)
    pl.semaphore_wait(barrier, n_sub - 1 + neighbours)
    copies = spread(0)

    for load in loads[4:]:
        load.wait()
    points, functions = values.shape
    elements = temps.shape[1]
    g3 = grads[...].reshape(3 * points, functions)
    g_head, g_rest = halves(jnp.concatenate([g3, values[...]], axis=0))
    left = jnp.concatenate([g_head, g_head, g_rest, g_rest], axis=1).astype(BF16)
    h3, l3 = g_head[: 3 * points], g_rest[: 3 * points]
    back = jnp.transpose(jnp.concatenate([h3, h3, l3, l3], axis=0)).astype(BF16)
    t_head, t_rest = halves(temps[...])
    four = jnp.concatenate([t_head, t_rest, t_head, t_rest], axis=0).astype(BF16)
    fields = dot(left, four)
    vals = fields[3 * points :]
    w = weights[...]
    terms[pl.ds(0, points), :] = w * CONDUCTIVITY * (1.0 + vals * vals)
    slope_weight = w * (2.0 * CONDUCTIVITY) * vals
    for c in range(3):
        terms[pl.ds((c + 1) * points, points), :] = (
            slope_weight * fields[c * points : (c + 1) * points]
        )
    block, col, quad = owner[...], column[...], quadrant[...]
    o = block >> log2(nbd)
    near = col - nbd
    far = near - n_sub * gh
    side = far >> log2(ig)
    own_place = o * erows + col
    near_place = (near >> log2(gh)) * erows + nbd + o * gh + (near & (gh - 1))
    far_place = 2 * base + (side * n_sub + o) * 2 * ig + (1 - side) * ig + (far & (ig - 1))
    neighbour = patch - 1 + 2 * side
    far_place = jnp.where((neighbour >= 0) & (neighbour < n_patch), far_place, -4 * (base + ifp))
    place = jnp.where(near < 0, own_place, jnp.where(far < 0, near_place, far_place))
    place = place + (quad & 1) * jnp.where(far < 0, base, ifp)
    active = lax.broadcasted_iota(jnp.int32, (1, elements), 1) < counts[...]
    target = jnp.where(active, block + (quad >> 1) * rbp, -1)
    for i in range(2 * (base + ifp) // 128):
        index = lax.broadcasted_iota(jnp.int32, (128, elements), 0) + i * 128
        pick[pl.ds(i * 128, 128), :] = jnp.where(index == place, 1.0, 0.0).astype(BF16)
    for i in range(2 * rbp // 128):
        index = lax.broadcasted_iota(jnp.int32, (128, elements), 0) + i * 128
        put[pl.ds(i * 128, 128), :] = jnp.where(index == target, 1.0, 0.0).astype(BF16)

    for sweep in range(SWEEPS - 1):
        gathered(sweep)
        x = dot(segments(sweep, 0, base), pick[pl.ds(0, 2 * base), :])
        gathered_far(sweep)
        x = x + dot(segments(sweep, base, ifp), pick[pl.ds(2 * base, 2 * ifp), :])
        x = x.astype(BF16)
        gx = dot(left, jnp.concatenate([x, x], axis=0))
        vx = gx[3 * points :]
        k0 = terms[pl.ds(0, points), :]
        flux = jnp.concatenate(
            [
                k0 * gx[c * points : (c + 1) * points]
                + terms[pl.ds((c + 1) * points, points), :] * vx
                for c in range(3)
            ],
            axis=0,
        )
        f_head, f_rest = halves(flux)
        z = dot_nt(jnp.concatenate([f_head, f_rest], axis=0).astype(BF16), put[...])
        z_head, z_rest = halves(z[: 3 * points] + z[3 * points :])
        rt = dot(back, jnp.concatenate([z_head, z_rest, z_head, z_rest], axis=0).astype(BF16))
        rows_out[sweep] = jnp.transpose(jnp.concatenate([rt[:, :rbp], rt[:, rbp:]], axis=0))
        for k, peer in enumerate(peers):
            copy = pltpu.make_async_remote_copy(
                src_ref=rows_out.at[sweep, pl.ds(pl.multiple_of(peer * nbd, 8), nbd)],
                dst_ref=rows_in.at[sweep, sub],
                send_sem=rs_send.at[sweep, k],
                recv_sem=rs_recv.at[sweep, sub],
                device_id=(patch, peer),
                device_id_type=MESH,
            )
            copy.start()
            copies.append(copy)
        for copy in copies:
            copy.wait_send()
        far_each(sweep, lambda copy: copy.wait_send())
        applied = mass[...] * u + rows_out[sweep, pl.ds(pl.multiple_of(sub * nbd, 8), nbd), :]
        for k, source in enumerate(sources):
            pltpu.make_async_remote_copy(
                src_ref=rows_in.at[sweep, source],
                dst_ref=rows_in.at[sweep, source],
                send_sem=rs_send.at[sweep, k],
                recv_sem=rs_recv.at[sweep, source],
                device_id=(patch, source),
                device_id_type=MESH,
            ).wait_recv()
            applied = applied + rows_in[sweep, source]
        u = u + solve(r - applied)
        if sweep < SWEEPS - 2:
            expand(u, sweep + 1)
            copies = spread(sweep + 1)
    out[...] = u


def body(
    element_temps,
    quad_weights,
    basis_values,
    basis_grads,
    owner_block,
    column_ref,
    quadrant,
    active_counts,
    send_list,
    iface_list,
    newton_residual,
    lumped_mass,
    precond,
):
    n_patch, n_sub = lax.axis_size("patch"), lax.axis_size("sub")
    nbd, points = newton_residual.shape
    gh, ig = send_list.shape[1], iface_list.shape[1]
    elements = element_temps.shape[0]
    quads = basis_values.shape[0]
    erows = -(-(nbd + n_sub * gh) // 8) * 8
    base = -(-(n_sub * erows) // 128) * 128
    ifp = -(-(4 * ig * n_sub) // 128) * 128
    nbp = base + ifp
    rbp = -(-(n_sub * nbd) // 128) * 128
    dims = (n_patch, n_sub, nbd, gh, ig, erows, base, ifp, rbp)
    steps = SWEEPS - 1
    vmem = pl.BlockSpec(memory_space=pltpu.VMEM)
    hbm = pl.BlockSpec(memory_space=pltpu.HBM)
    dma = pltpu.SemaphoreType.DMA
    return pl.pallas_call(
        functools.partial(kernel, dims),
        out_shape=jax.ShapeDtypeStruct((nbd, points), F32),
        in_specs=[hbm] * 13,
        out_specs=vmem,
        scratch_shapes=[
            pltpu.VMEM(element_temps.shape[::-1], F32),
            pltpu.VMEM(quad_weights.shape[::-1], F32),
            pltpu.VMEM(basis_values.shape, F32),
            pltpu.VMEM(basis_grads.shape, F32),
            pltpu.VMEM((1, elements), jnp.int32),
            pltpu.VMEM((1, elements), jnp.int32),
            pltpu.VMEM((1, elements), jnp.int32),
            pltpu.VMEM((1, 1), jnp.int32),
            pltpu.SMEM(send_list.shape[::-1], jnp.int32),
            pltpu.SMEM(iface_list.shape, jnp.int32),
            pltpu.VMEM(newton_residual.shape, F32),
            pltpu.VMEM(lumped_mass.shape, F32),
            pltpu.VMEM(precond.shape, F32),
            dma((13,)),
            pltpu.VMEM((steps, nbp, points), F32),
            pltpu.VMEM((steps, 2 * ig, points), F32),
            pltpu.VMEM((steps, rbp, points), F32),
            pltpu.VMEM((steps, n_sub, nbd, points), F32),
            pltpu.VMEM((2 * nbp, elements), BF16),
            pltpu.VMEM((2 * rbp, elements), BF16),
            pltpu.VMEM((4 * quads, elements), F32),
            pltpu.VMEM((nbd * points, points), BF16),
            pltpu.VMEM((nbd * points, points), BF16),
            dma((steps, n_sub)),
            dma((steps, n_sub)),
            dma((steps, 2, n_sub)),
            dma((steps, 2, n_sub)),
            dma((steps, n_sub)),
            dma((steps, n_sub)),
        ],
        compiler_params=pltpu.CompilerParams(
            collective_id=0, has_side_effects=True, vmem_limit_bytes=56 * 1024 * 1024
        ),
    )(
        element_temps.T,
        quad_weights.T,
        basis_values,
        basis_grads,
        owner_block.reshape(1, elements),
        column_ref.reshape(1, elements),
        quadrant.reshape(1, elements),
        active_counts.reshape(1, 1),
        send_list.T,
        iface_list,
        newton_residual,
        lumped_mass,
        precond,
    )


def solution(mesh):
    return jax.shard_map(
        body,
        mesh=mesh,
        in_specs=(
            P(("patch", "sub"), None),
            P(("patch", "sub"), None),
            P(),
            P(),
            P(("patch", "sub"), None),
            P(("patch", "sub"), None),
            P(("patch", "sub"), None),
            P(("patch", "sub")),
            P(("patch", "sub"), None),
            P(("patch", "sub"), None),
            P(("patch", "sub"), None),
            P(("patch", "sub"), None),
            P(("patch", "sub"), None, None),
        ),
        out_specs=P(("patch", "sub"), None),
        check_vma=False,
    )
```
